256 devices in a mesh: rows: 128 (over x, z, y_hi, core), heads: 2 (over y_lo).
Axes of the slice: x: 4, y: 4 (y_hi: 2, y_lo: 2; y = y_hi * 2 + y_lo), z: 8, core: 2. Of those that a mesh axis runs over, the one named last changes fastest.
Arguments:
- queries: bfloat16 [256, 4, 32, 1024], P('rows', 'heads'), may hold values from -6 to 6
- keys: bfloat16 [256, 4, 32, 1024], P('rows', 'heads'), may hold values from -6 to 6
- values: bfloat16 [256, 4, 32, 1024], P('rows', 'heads'), may hold values from -6 to 6
- d_out: bfloat16 [256, 4, 32, 1024], P('rows', 'heads'), may hold values from -24 to 24
- bias: bfloat16 [4, 1024, 1024], P('heads', 'rows'), may hold values from -4 to 400, as said below
- w_bias: bfloat16 [128, 4], replicated, may hold values from -96 to 96
Outputs:
- d_queries: bfloat16 [256, 4, 32, 1024], P('rows', 'heads')
- d_keys: bfloat16 [256, 4, 32, 1024], P('rows', 'heads')
- d_values: bfloat16 [256, 4, 32, 1024], P('rows', 'heads')
- d_pair: bfloat16 [1024, 1024, 128], P('rows', 'heads')
The draws below stay inside these ranges and needn't reach their ends.
Inputs may be any that keep to these rules, and one draw needn't show every extreme that they name: bias entries stay within the stated bounds.
All inputs are finite; a program needn't handle non-finite values.
Results may differ from the reference program's by a relative error of at most 0.0051.
Values may be sent and summed in bfloat16 or wider, within the bound.
No kernel may reach another device: no remote copies, remote signals or barrier semaphores. Data moves between devices by JAX's collectives and lax.ppermute only.
A program may use at most 64 MiB of HBM per device.

```python
import jax
import jax.numpy as jnp
from jax import lax

C = 128
H = 4
D = 32
L = 1024
ROWS = 256


def draw_bias(key, part):
    key_base = jax.random.fold_in(key, 11)
    base = jnp.clip(jax.random.normal(key_base, (H, L, L), jnp.float32), -4.0, 4.0)
    return base.astype(jnp.bfloat16)


def with_spikes(entries, own_key, source, target, blocks, factor):
    def block_of(axis_at):
        return (jnp.arange(entries.shape[axis_at]) // (entries.shape[axis_at] // blocks)).reshape((-1,) + (1,) * (entries.ndim - 1 - axis_at))

    near = jax.random.permutation(own_key, blocks)[block_of(target)]
    second = (block_of(target) + blocks // 2) % blocks
    return jnp.where((block_of(source) == near) | (block_of(source) == second), factor * entries, entries)


def shard_levels(rng, dims, cuts, low, high):
    level = 1.0
    for position, shards_of in cuts:
        draws = jax.random.uniform(jax.random.fold_in(jax.random.fold_in(rng, 6), position), (shards_of,), jnp.float32, low / len(cuts), high / len(cuts))
        level = level * jnp.repeat(jnp.exp(draws), dims[position] // shards_of).reshape((-1,) + (1,) * (len(dims) - 1 - position))
    return level


def bell_draw(own_key, extent, width, bound, pieces=(), dtype=jnp.bfloat16):
    entries = jax.random.normal(own_key, extent, jnp.float32) * width
    if len(pieces) > 0:
        entries = shard_levels(own_key, extent, pieces, -0.22, 0.18) * entries
    return jnp.clip(entries, min=-bound, max=bound).astype(dtype)


def heavy_noise(own_key, shape, scale, most, cuts, heavy, dtype=jnp.bfloat16):
    drawn = scale * jax.random.normal(own_key, shape, jnp.float32)
    if cuts:
        drawn = drawn * shard_levels(own_key, shape, cuts, -0.22, 0.18)
    return jnp.clip(with_spikes(drawn, jax.random.fold_in(own_key, 3), *heavy), -most, most).astype(dtype)


def setup_inputs(seed: int = 0) -> dict:
    key_of = jax.random.split(jax.random.key(seed), 7)
    return {
        "queries": bell_draw(key_of[0], (ROWS, H, D, L), 1.0, 6.0, ((0, 128), (1, 2))),
        "keys": bell_draw(key_of[1], (ROWS, H, D, L), 1.0, 6.0, ((0, 128), (1, 2))),
        "values": bell_draw(key_of[2], (ROWS, H, D, L), 1.0, 6.0, ((0, 128), (1, 2))),
        "d_out": heavy_noise(key_of[3], (ROWS, H, D, L), 1.0, 24.0, ((0, 128), (1, 2)), (0, 3, 128, 5.5)),
        "bias": draw_bias(jax.random.fold_in(key_of[6], 71), 0),
        "w_bias": bell_draw(key_of[5], (C, H), 16.0, 96.0),
    }


def reference(queries, keys, values, d_out, bias, w_bias):
    scale = D ** -0.5
    bias_f = bias.astype(jnp.float32)

    def step(d_bias, items):
        q_row, k_row, v_row, g_row = [t.astype(jnp.float32) for t in items]
        scores = jnp.einsum('hdq,hdk->hqk', q_row, k_row) * scale + bias_f
        top = jnp.max(scores, axis=-1, keepdims=True)
        expo = jnp.exp(scores - top)
        probs = expo / jnp.sum(expo, axis=-1, keepdims=True)
        d_probs = jnp.einsum('hdq,hdk->hqk', g_row, v_row)
        d_scores = probs * (d_probs - jnp.sum(probs * d_probs, axis=-1, keepdims=True))
        probs_low = lax.optimization_barrier(probs.astype(jnp.bfloat16)).astype(jnp.float32)
        d_low = lax.optimization_barrier(d_scores.astype(jnp.bfloat16)).astype(jnp.float32)
        grad_q = jnp.einsum('hqk,hdk->hdq', d_low, k_row) * scale
        grad_k = jnp.einsum('hqk,hdq->hdk', d_low, q_row) * scale
        grad_v = jnp.einsum('hqk,hdq->hdk', probs_low, g_row)
        return d_bias + d_scores, (grad_q.astype(jnp.bfloat16), grad_k.astype(jnp.bfloat16), grad_v.astype(jnp.bfloat16))

    start_bias = jnp.zeros((H, L, L), jnp.float32)
    d_bias, grads = lax.scan(step, start_bias, (queries, keys, values, d_out))
    d_pair = jnp.einsum('hjk,ch->jkc', d_bias, w_bias.astype(jnp.float32), precision=lax.Precision.HIGHEST)
    return grads[0], grads[1], grads[2], d_pair.astype(jnp.bfloat16)
```

```python
import functools
import math

import jax
import jax.numpy as jnp
from jax import lax
from jax.experimental import pallas as pl
from jax.experimental.pallas import tpu as pltpu
from jax.sharding import PartitionSpec as P

NX, NZ, NY, NC, NH = 4, 8, 2, 2, 2
AXES = ("rows", "heads")
LOG2E = 1.4426950408889634
BF = jnp.bfloat16
F32 = jnp.float32
JB = 256
STRIP = 16


def send(value, dx=0, dz=0, dy=0, dc=0, dh=0):
    pairs = []
    for x in range(NX):
        for z in range(NZ):
            for y in range(NY):
                for c in range(NC):
                    for h in range(NH):
                        def flat(x, z, y, c, h):
                            return (((x * NZ + z) * NY + y) * NC + c) * NH + h
                        pairs.append((
                            flat(x, z, y, c, h),
                            flat((x + dx) % NX, (z + dz) % NZ, (y + dy) % NY, (c + dc) % NC, (h + dh) % NH),
                        ))
    return lax.ppermute(value, AXES, pairs)


def split3(value):
    hi = value.astype(BF)
    rest = value - hi.astype(F32)
    mid = rest.astype(BF)
    low = (rest - mid.astype(F32)).astype(BF)
    return hi, mid, low


def row_start(place, dx, dz, e, core):
    x, z, y = place[0], place[1], place[2]
    return ((x - dx) & (NX - 1)) * 256 + ((z - dz) & (NZ - 1)) * 32 + (y ^ e) * 16 + core * 8


def attention_kernel(scale, place, qkvg, *refs):
    bias_refs = refs[: 2 * NX]
    grads, out_send, out_own = refs[2 * NX : 2 * NX + 3]
    bias_f, total, s_buf, p_buf, pl_buf, dl_buf, gk, gv = refs[2 * NX + 3 :]
    row, block = pl.program_id(0), pl.program_id(1)
    length = bias_f.shape[1]

    @pl.when((row == 0) & (block == 0))
    def _():
        def place_one(t, carry):
            dz, e = t // 2, t % 2
            for dx in range(NX):
                for cc in range(NC):
                    start = row_start(place, dx, dz, e, place[3] ^ cc)
                    piece = bias_refs[cc * NX + dx][dz, e].astype(F32) * LOG2E
                    bias_f[pl.ds(pl.multiple_of(start, 8), 8), :] = piece
            return carry
        lax.fori_loop(0, NZ * NY, place_one, 0)
        total[...] = jnp.zeros_like(total)

    cols = pl.ds(pl.multiple_of(block * JB, JB), JB)
    q = qkvg[0, 0, :, cols]
    k = qkvg[1, 0]
    v = qkvg[2, 0]
    g = qkvg[3, 0, :, cols]
    q3 = jnp.concatenate(split3(q.astype(F32) * (scale * LOG2E)), axis=0)
    k3 = jnp.concatenate([k, k, k], axis=0)
    over_rows = (((0,), (0,)), ((), ()))
    over_cols = (((1,), (1,)), ((), ()))
    s_buf[...] = lax.dot_general(q3, k3, over_rows, preferred_element_type=F32)
    p_buf[...] = lax.dot_general(g, v, over_rows, preferred_element_type=F32)

    def strip(i, carry):
        here = pl.ds(pl.multiple_of(i * STRIP, STRIP), STRIP)
        there = pl.ds(pl.multiple_of(block * JB + i * STRIP, STRIP), STRIP)
        s = s_buf[here, :] + bias_f[there, :]
        top = jnp.max(s, axis=1, keepdims=True)
        expo = jnp.exp2(s - top)
        inv = 1.0 / jnp.sum(expo, axis=1, keepdims=True)
        dp = p_buf[here, :]
        mean = jnp.sum(expo * dp, axis=1, keepdims=True) * inv
        probs = expo * inv
        ds = probs * (dp - mean)
        pl_buf[here, :] = probs.astype(BF)
        dl_buf[here, :] = ds.astype(BF)
        total[there, :] += ds
        return carry

    lax.fori_loop(0, JB // STRIP, strip, 0, unroll=2)

    d_low = dl_buf[...]
    p_low = pl_buf[...]
    gq = lax.dot_general(k, d_low, over_cols, preferred_element_type=F32) * scale
    grads[0, 0, :, cols] = gq.astype(BF)
    new_k = jnp.dot(q, d_low, preferred_element_type=F32)
    new_v = jnp.dot(g, p_low, preferred_element_type=F32)

    @pl.when(block == 0)
    def _():
        gk[...] = new_k
        gv[...] = new_v

    @pl.when(block > 0)
    def _():
        gk[...] += new_k
        gv[...] += new_v

    @pl.when(block == length // JB - 1)
    def _():
        grads[1, 0] = (gk[...] * scale).astype(BF)
        grads[2, 0] = gv[...].astype(BF)

    @pl.when((row == pl.num_programs(0) - 1) & (block == length // JB - 1))
    def _():
        def take_one(t, carry):
            dz, e = t // 2, t % 2
            for dx in range(NX):
                mine = row_start(place, dx, dz, e, place[3])
                other = row_start(place, dx, dz, e, place[3] ^ 1)
                out_own[dx, dz, e] = total[pl.ds(pl.multiple_of(mine, 8), 8), :]
                out_send[dx, dz, e] = total[pl.ds(pl.multiple_of(other, 8), 8), :].astype(BF)
            return carry
        lax.fori_loop(0, NZ * NY, take_one, 0)


def attention(place, qkvg, bias_parts, scale):
    _, rows, depth, length = qkvg.shape
    blocks = length // JB
    part = (NX, NZ, NY, 8, length)
    whole = lambda *shape: pl.BlockSpec(shape, lambda r, b: (0,) * len(shape))
    return pl.pallas_call(
        functools.partial(attention_kernel, scale),
        grid=(rows, blocks),
        out_shape=(
            jax.ShapeDtypeStruct((3, rows, depth, length), BF),
            jax.ShapeDtypeStruct(part, BF),
            jax.ShapeDtypeStruct(part, F32),
        ),
        in_specs=[
            pl.BlockSpec(memory_space=pltpu.SMEM),
            pl.BlockSpec((4, 1, depth, length), lambda r, b: (0, r, 0, 0)),
        ] + [whole(NZ, NY, 8, length)] * (2 * NX),
        out_specs=(
            pl.BlockSpec((3, 1, depth, length), lambda r, b: (0, r, 0, 0)),
            whole(*part),
            whole(*part),
        ),
        scratch_shapes=[
            pltpu.VMEM((length, length), F32),
            pltpu.VMEM((length, length), F32),
            pltpu.VMEM((JB, length), F32),
            pltpu.VMEM((JB, length), F32),
            pltpu.VMEM((JB, length), BF),
            pltpu.VMEM((JB, length), BF),
            pltpu.VMEM((depth, length), F32),
            pltpu.VMEM((depth, length), F32),
        ],
        compiler_params=pltpu.CompilerParams(
            vmem_limit_bytes=48 * 1024 * 1024,
            dimension_semantics=("arbitrary", "arbitrary"),
        ),
        cost_estimate=pl.CostEstimate(flops=10_000_000_000, bytes_accessed=8_000_000, transcendentals=4_000_000),
        name="attention_backward",
    )(place, qkvg, *bias_parts)


def pair_kernel(terms, weight, out):
    heads, rows, width = terms.shape
    for j in range(rows):
        parts = [piece for piece in split3(terms[:, j, :])]
        lhs = jnp.concatenate([p.astype(F32) for p in parts], axis=0)
        lhs = jnp.concatenate([lhs, jnp.zeros((16 - 3 * heads, width), F32)], axis=0).astype(BF)
        out[j] = lax.dot_general(
            lhs, weight[...], (((0,), (0,)), ((), ())), preferred_element_type=F32
        ).astype(BF)


def pair_gradient(terms, weight):
    heads, rows, width = terms.shape
    return pl.pallas_call(
        pair_kernel,
        out_shape=jax.ShapeDtypeStruct((rows, width, weight.shape[1]), BF),
        name="pair_gradient",
    )(terms, weight)


def shards(queries, keys, values, d_out, bias, w_bias):
    _, _, depth, length = queries.shape
    scale = depth ** (-0.5)
    r = lax.axis_index("rows")
    h = lax.axis_index("heads")
    x, z, y, c = r // 32, (r // 4) % 8, (r // 2) % 2, r % 2
    place = jnp.stack([x, z, y, c]).astype(jnp.int32)

    keep = lax.dynamic_index_in_dim(bias, y, 0, keepdims=False)
    give = lax.dynamic_index_in_dim(bias, 1 - y, 0, keepdims=False)
    got = send(give, dy=1)
    both = jnp.stack([keep, got])
    all_in = jnp.stack([queries, keys, values, d_out])
    own_in = lax.dynamic_index_in_dim(all_in, y, 2, keepdims=False)
    got_in = send(lax.dynamic_index_in_dim(all_in, 1 - y, 2, keepdims=False), dy=1)
    qkvg = jnp.concatenate([own_in, got_in], axis=1)

    along_z = jnp.stack([both] + [send(both, dz=d) for d in range(1, NZ)])
    along_x = [along_z] + [send(along_z, dx=d) for d in range(1, NX)]
    bias_parts = along_x + [send(part, dc=1) for part in along_x]

    grads, other, own = attention(place, qkvg, bias_parts, scale)

    chip = own + send(other, dc=1).astype(F32)
    low = chip.astype(BF)
    plane = chip[0]
    for d in range(1, NX):
        plane = plane + send(low[d], dx=-d).astype(F32)
    low = plane.astype(BF)
    line = plane[0]
    for d in range(1, NZ):
        line = line + send(low[d], dz=-d).astype(F32)

    half = length // NH
    lines = line.reshape(NY, 8, NH, half)
    terms = []
    ids = []
    for dy in range(NY):
        for dh in range(NH):
            piece = lax.dynamic_index_in_dim(lines[dy], h ^ dh, 1, keepdims=False)
            terms.append(send(piece, dy=dy, dh=dh) if dy or dh else piece)
            ids.append(2 * (h ^ dh) + (y ^ dy))
    weight = w_bias.T[jnp.stack(ids)]
    weight = jnp.concatenate([weight, weight, weight, jnp.zeros_like(weight)], axis=0)
    d_pair = pair_gradient(jnp.stack(terms), weight)

    back = send(grads[:, 2:], dy=1)
    mine = grads[:, :2]
    first = jnp.where(y == 0, mine, back)
    second = jnp.where(y == 0, back, mine)
    outs = jnp.stack([first, second], axis=2)
    return outs[0], outs[1], outs[2], d_pair


def solution(mesh):
    return jax.shard_map(
        shards,
        mesh=mesh,
        in_specs=(
            P("rows", "heads", None, None),
            P("rows", "heads", None, None),
            P("rows", "heads", None, None),
            P("rows", "heads", None, None),
            P("heads", "rows", None),
            P(),
        ),
        out_specs=(
            P("rows", "heads", None, None),
            P("rows", "heads", None, None),
            P("rows", "heads", None, None),
            P("rows", "heads", None),
        ),
        check_vma=False,
    )
```

```python
import functools

import jax
import jax.numpy as jnp
from jax import lax
from jax.experimental import pallas as pl
from jax.experimental.pallas import tpu as pltpu
from jax.sharding import Mesh, PartitionSpec as P

NX, NZ, NY, NC, NH = 4, 8, 2, 2, 2
GRID = ("x", "z", "yh", "core", "heads")
ROWS = ("x", "z", "yh", "core")
COST = 4_600_000_000
LOG2E = 1.4426950408889634
BF = jnp.bfloat16
F32 = jnp.float32
OVER_ROWS = (((0,), (0,)), ((), ()))
OVER_COLS = (((1,), (1,)), ((), ()))


def shift(value, axis, size, by):
    return lax.ppermute(value, axis, [(i, (i + by) % size) for i in range(size)])


def split3(value):
    hi = value.astype(BF)
    rest = value - hi.astype(F32)
    mid = rest.astype(BF)
    low = (rest - mid.astype(F32)).astype(BF)
    return hi, mid, low


def chunk_kernel(scale, first, last, place, q_ref, k_ref, v_ref, g_ref, mine, sibling, *refs):
    if first:
        old_k = old_v = None
    else:
        old_k, old_v, _ = refs[:3]
        refs = refs[3:]
    out_own, out_other, gk_ref, gv_ref, gq_ref = refs[:5]
    bias_f, total, s_buf, p_buf, pl_buf, dl_buf = refs[5:]
    core = place[1]
    rows, depth, width = q_ref.shape[1:]
    length = k_ref.shape[-1]
    pick = lambda ref: lambda r, cols=slice(None): ref[0, r, :, cols]
    q_at, k_at, v_at, g_at = pick(q_ref), pick(k_ref), pick(v_ref), pick(g_ref)
    tiles = length // 256
    groups = width // 16

    for n in range(groups):
        bias_f[n, core] = mine[n].astype(F32) * LOG2E
        bias_f[n, 1 - core] = sibling[n].astype(F32) * LOG2E

    held = {}

    def scores(r, t):
        if t == 0:
            q3 = jnp.concatenate(split3(q_at(r).astype(F32) * (scale * LOG2E)), axis=0)
            k = k_at(r)
            held[r] = (q3, jnp.concatenate([k, k, k], axis=0))
        cols = slice(256 * (t % tiles), 256 * (t % tiles) + 256)
        if t < tiles:
            s_buf[r % 2, :, cols] = lax.dot_general(
                held[r][0], held[r][1][:, cols], OVER_ROWS, preferred_element_type=F32
            )
        else:
            p_buf[r % 2, :, cols] = lax.dot_general(
                g_at(r), v_at(r, cols), OVER_ROWS, preferred_element_type=F32
            )

    sums = {}

    def gradients(r, t):
        cols = slice(256 * (t % tiles), 256 * (t % tiles) + 256)
        if t < tiles:
            new = jnp.dot(q_at(r), dl_buf[r % 2, :, cols], preferred_element_type=F32)
            if old_k is not None:
                new = old_k[r, :, cols] + new
            gk_ref[r, :, cols] = (new * scale).astype(BF) if last else new
        elif t < 2 * tiles:
            new = jnp.dot(g_at(r), pl_buf[r % 2, :, cols], preferred_element_type=F32)
            if old_v is not None:
                new = old_v[r, :, cols] + new
            gv_ref[r, :, cols] = new.astype(BF) if last else new
        else:
            new = lax.dot_general(
                k_at(r, cols), dl_buf[r % 2, :, cols], OVER_COLS, preferred_element_type=F32
            )
            sums[r] = sums[r] + new if r in sums else new
            if t == 3 * tiles - 1:
                gq_ref[r] = (sums[r] * scale).astype(BF)

    def softmax(r, n):
        here = slice(16 * n, 16 * n + 16)
        s = s_buf[r % 2, here, :] + bias_f[n].reshape(16, length)
        top = jnp.max(s, axis=1, keepdims=True)
        expo = jnp.exp2(s - top)
        inv = 1.0 / jnp.sum(expo, axis=1, keepdims=True)
        dp = p_buf[r % 2, here, :]
        mean = jnp.sum(expo * dp, axis=1, keepdims=True) * inv
        probs = expo * inv
        ds = probs * (dp - mean)
        pl_buf[r % 2, here, :] = probs.astype(BF)
        dl_buf[r % 2, here, :] = ds.astype(BF)
        split = ds.reshape(2, 8, length)
        if r == 0:
            total[n] = split
        else:
            total[n] += split

    for step in range(rows + 2):
        matmuls = []
        if step < rows:
            matmuls += [(scores, step, t) for t in range(2 * tiles)]
        if step >= 2:
            matmuls += [(gradients, step - 2, t) for t in range(3 * tiles)]
        if 0 <= step - 1 < rows:
            for n in range(groups):
                for f, r, t in matmuls[len(matmuls) * n // groups : len(matmuls) * (n + 1) // groups]:
                    f(r, t)
                softmax(step - 1, n)
        else:
            for f, r, t in matmuls:
                f(r, t)

    for n in range(groups):
        out_own[n] = total[n, core]
        out_other[n] = total[n, 1 - core].astype(BF)


def chunk(place, qkvg, mine, sibling, held, last, scale):
    _, rows, depth, length = qkvg.shape
    groups = mine.shape[0]
    width = 16 * groups
    first = held is None
    narrow = lambda i: pl.BlockSpec((1, rows, depth, width), lambda g, p: (i, 0, 0, p[0]))
    wide = lambda i: pl.BlockSpec((1, rows, depth, length), lambda g, p: (i, 0, 0, 0))
    whole = lambda *shape: pl.BlockSpec(shape, lambda g, p: (0,) * len(shape))
    part = whole(groups, 8, length)
    sums = whole(rows, depth, length)
    out_type = BF if last else F32
    extra = [] if first else list(held)
    return pl.pallas_call(
        functools.partial(chunk_kernel, scale, first, last),
        grid_spec=pltpu.PrefetchScalarGridSpec(
            num_scalar_prefetch=1,
            grid=(1,),
            in_specs=[narrow(0), wide(1), wide(2), narrow(3), part, part]
            + ([] if first else [sums, sums, pl.BlockSpec(memory_space=pl.ANY)]),
            out_specs=(
                whole(groups, 8, length),
                whole(groups, 8, length),
                sums,
                sums,
                pl.BlockSpec((rows, depth, width), lambda g, p: (0, 0, p[0])),
            ),
            scratch_shapes=[
                pltpu.VMEM((groups, 2, 8, length), F32),
                pltpu.VMEM((groups, 2, 8, length), F32),
                pltpu.VMEM((2, width, length), F32),
                pltpu.VMEM((2, width, length), F32),
                pltpu.VMEM((2, width, length), BF),
                pltpu.VMEM((2, width, length), BF),
            ],
        ),
        out_shape=(
            jax.ShapeDtypeStruct((groups, 8, length), F32),
            jax.ShapeDtypeStruct((groups, 8, length), BF),
            jax.ShapeDtypeStruct((rows, depth, length), out_type),
            jax.ShapeDtypeStruct((rows, depth, length), out_type),
            jax.ShapeDtypeStruct((rows, depth, length), BF),
        ),
        input_output_aliases={} if first else ({9: 4} if last else {7: 2, 8: 3, 9: 4}),
        compiler_params=pltpu.CompilerParams(vmem_limit_bytes=24 * 1024 * 1024),
        cost_estimate=pl.CostEstimate(flops=COST, bytes_accessed=4_000_000, transcendentals=0),
        name="attention_chunk",
    )(place, qkvg, qkvg, qkvg, qkvg, mine, sibling, *extra)


def plane_kernel(own, got, one, two, three, out):
    half = out.shape[-1]
    for n in range(out.shape[0]):
        s = own[n] + got[n].astype(F32)
        s = s + one[n].astype(F32) + two[n].astype(F32) + three[n].astype(F32)
        low = s.astype(BF)
        for h in range(NH):
            out[n, h] = low[:, h * half : (h + 1) * half]


def plane_sum(own, got, arrived):
    groups, eight, length = own.shape
    return pl.pallas_call(
        plane_kernel,
        out_shape=jax.ShapeDtypeStruct((groups, NH, eight, length // NH), BF),
        compiler_params=pltpu.CompilerParams(vmem_limit_bytes=8 * 1024 * 1024),
        name="plane_sum",
    )(own, got, *arrived)


def pair_kernel(terms, weight, out):
    width = terms.shape[-1]
    heads = []
    for y in range(NY):
        for h in range(NH):
            s = terms[0, y, h].astype(F32)
            for z in range(1, NZ):
                s = s + terms[z, y, h].astype(F32)
            heads.append(split3(s))
    pad = jnp.zeros((4, width), F32)
    for j in range(out.shape[0]):
        lhs = [heads[i][p][j : j + 1, :].astype(F32) for p in range(3) for i in range(4)]
        lhs = jnp.concatenate(lhs + [pad], axis=0).astype(BF)
        out[j] = lax.dot_general(lhs, weight[...], OVER_ROWS, preferred_element_type=F32).astype(BF)


def pair_gradient(terms, weight):
    return pl.pallas_call(
        pair_kernel,
        out_shape=jax.ShapeDtypeStruct((terms.shape[3], terms.shape[4], weight.shape[1]), BF),
        compiler_params=pltpu.CompilerParams(vmem_limit_bytes=8 * 1024 * 1024),
        name="pair_gradient",
    )(terms, weight)


def shards(queries, keys, values, d_out, bias, w_bias):
    _, _, depth, length = queries.shape
    scale = depth ** (-0.5)
    x, y, c = lax.axis_index("x"), lax.axis_index("yh"), lax.axis_index("core")

    all_in = (queries, keys, values, d_out)
    pick = lambda at: jnp.stack([lax.dynamic_index_in_dim(t, at, 1, keepdims=False) for t in all_in])
    got_in = shift(pick(1 - y), "yh", NY, 1)

    spread = jnp.broadcast_to(bias[None], (NZ,) + bias.shape).reshape(NZ * NY, 8, length)
    own_bias = lax.all_to_all(spread, ("z", "yh"), 0, 0, tiled=True)
    own_bias, got_in = lax.optimization_barrier((own_bias, got_in))
    qkvg = jnp.concatenate([pick(y), got_in], axis=1)
    order = (0, 1, 3, 2)
    halves = [shift(own_bias, "x", NX, dx) if dx else own_bias for dx in order]

    held = None
    arrived = []
    for at, dx in enumerate(order):
        mine = halves[at]
        if at == 1:
            mine = lax.optimization_barrier((mine, plane_own))[0]
        sibling = shift(mine, "core", NC, 1)
        place = jnp.stack([(x + NX - dx) % NX, c]).astype(jnp.int32)
        own, other, *held = chunk(place, qkvg, mine, sibling, held, at == len(order) - 1, scale)
        got = shift(other, "core", NC, 1)
        if dx:
            arrived.append(shift((own + got.astype(F32)).astype(BF), "x", NX, -dx))
        else:
            plane_own, plane_got = own, got
    gk, gv, gq = held

    plane = plane_sum(plane_own, plane_got, arrived)
    plane = plane.reshape(NZ * NY * NH, 8, length // NH)
    terms = lax.all_to_all(plane, ("z", "yh", "heads"), 0, 0, tiled=True)
    terms = terms.reshape(NZ, NY, NH, 8, length // NH)
    weight = jnp.stack([w_bias[:, 2 * h + y] for y in range(NY) for h in range(NH)])
    weight = jnp.concatenate([weight, weight, weight, jnp.zeros_like(weight)], axis=0)
    d_pair = pair_gradient(terms, weight)

    grads = jnp.stack([gq, gk, gv])
    back = shift(grads[:, 2:], "yh", NY, 1)
    mine = grads[:, :2]
    first = jnp.where(y == 0, mine, back)
    second = jnp.where(y == 0, back, mine)
    outs = jnp.stack([first, second], axis=2)
    return outs[0], outs[1], outs[2], d_pair


def solution(mesh):
    fine = Mesh(mesh.devices.reshape(NX, NZ, NY, NC, NH), GRID)
    block = P(ROWS, "heads", None, None)
    return jax.shard_map(
        shards,
        mesh=fine,
        in_specs=(block, block, block, block, P("heads", ROWS, None), P()),
        out_specs=(block, block, block, P(ROWS, "heads", None)),
        check_vma=False,
    )
```

```python
import functools

import jax
import jax.numpy as jnp
from jax import lax
from jax.experimental import pallas as pl
from jax.experimental.pallas import tpu as pltpu
from jax.sharding import Mesh, PartitionSpec as P

NX, NZ, NY, NC, NH = 4, 8, 2, 2, 2
GRID = ("x", "z", "yh", "core", "heads")
ROWS = ("x", "z", "yh", "core")
COST = 4_600_000_000
LOG2E = 1.4426950408889634
BF = jnp.bfloat16
F32 = jnp.float32
OVER_ROWS = (((0,), (0,)), ((), ()))
OVER_COLS = (((1,), (1,)), ((), ()))


def shift(value, axis, size, by):
    return lax.ppermute(value, axis, [(i, (i + by) % size) for i in range(size)])


def split3(value):
    hi = value.astype(BF)
    rest = value - hi.astype(F32)
    mid = rest.astype(BF)
    low = (rest - mid.astype(F32)).astype(BF)
    return hi, mid, low


def chunk_kernel(scale, place, q_ref, k_ref, v_ref, g_ref, mine, sibling,
                 out_own, out_other, gk_ref, gv_ref, gq_ref, bias_f, total, s_buf, p_buf, pl_buf, dl_buf):
    core = place[1]
    rows, depth, width = q_ref.shape[1:]
    length = k_ref.shape[-1]
    pick = lambda ref: lambda r, cols=slice(None): ref[0, r, :, cols]
    q_at, k_at, v_at, g_at = pick(q_ref), pick(k_ref), pick(v_ref), pick(g_ref)
    tiles = length // 256
    groups = width // 16

    for n in range(groups):
        bias_f[n, core] = mine[n].astype(F32) * LOG2E
        bias_f[n, 1 - core] = sibling[n].astype(F32) * LOG2E

    held = {}

    def scores(r, t):
        if t == 0:
            q3 = jnp.concatenate(split3(q_at(r).astype(F32) * (scale * LOG2E)), axis=0)
            k = k_at(r)
            held[r] = (q3, jnp.concatenate([k, k, k], axis=0))
        cols = slice(256 * (t % tiles), 256 * (t % tiles) + 256)
        if t < tiles:
            s_buf[r % 2, :, cols] = lax.dot_general(
                held[r][0], held[r][1][:, cols], OVER_ROWS, preferred_element_type=F32
            )
        else:
            p_buf[r % 2, :, cols] = lax.dot_general(
                g_at(r), v_at(r, cols), OVER_ROWS, preferred_element_type=F32
            )

    sums = {}

    def gradients(r, t):
        cols = slice(256 * (t % tiles), 256 * (t % tiles) + 256)
        if t < tiles:
            gk_ref[r, :, cols] = jnp.dot(q_at(r), dl_buf[r % 2, :, cols], preferred_element_type=F32)
        elif t < 2 * tiles:
            gv_ref[r, :, cols] = jnp.dot(g_at(r), pl_buf[r % 2, :, cols], preferred_element_type=F32)
        else:
            new = lax.dot_general(
                k_at(r, cols), dl_buf[r % 2, :, cols], OVER_COLS, preferred_element_type=F32
            )
            sums[r] = sums[r] + new if r in sums else new
            if t == 3 * tiles - 1:
                gq_ref[r] = (sums[r] * scale).astype(BF)

    def softmax(r, n):
        here = slice(16 * n, 16 * n + 16)
        s = s_buf[r % 2, here, :] + bias_f[n].reshape(16, length)
        top = jnp.max(s, axis=1, keepdims=True)
        expo = jnp.exp2(s - top)
        inv = 1.0 / jnp.sum(expo, axis=1, keepdims=True)
        dp = p_buf[r % 2, here, :]
        mean = jnp.sum(expo * dp, axis=1, keepdims=True) * inv
        probs = expo * inv
        ds = probs * (dp - mean)
        pl_buf[r % 2, here, :] = probs.astype(BF)
        dl_buf[r % 2, here, :] = ds.astype(BF)
        split = ds.reshape(2, 8, length)
        if r == 0:
            total[n] = split
        else:
            total[n] += split

    for step in range(rows + 2):
        matmuls = []
        if step < rows:
            matmuls += [(scores, step, t) for t in range(2 * tiles)]
        if step >= 2:
            matmuls += [(gradients, step - 2, t) for t in range(3 * tiles)]
        if 0 <= step - 1 < rows:
            for n in range(groups):
                for f, r, t in matmuls[len(matmuls) * n // groups : len(matmuls) * (n + 1) // groups]:
                    f(r, t)
                softmax(step - 1, n)
        else:
            for f, r, t in matmuls:
                f(r, t)

    for n in range(groups):
        out_own[n] = total[n, core]
        out_other[n] = total[n, 1 - core].astype(BF)


def chunk(place, qkvg, mine, sibling, scale):
    _, rows, depth, length = qkvg.shape
    groups = mine.shape[0]
    width = 16 * groups
    narrow = lambda i: pl.BlockSpec((1, rows, depth, width), lambda g, p: (i, 0, 0, p[0]))
    wide = lambda i: pl.BlockSpec((1, rows, depth, length), lambda g, p: (i, 0, 0, 0))
    whole = lambda *shape: pl.BlockSpec(shape, lambda g, p: (0,) * len(shape))
    part = whole(groups, 8, length)
    sums = whole(rows, depth, length)
    return pl.pallas_call(
        functools.partial(chunk_kernel, scale),
        grid_spec=pltpu.PrefetchScalarGridSpec(
            num_scalar_prefetch=1,
            grid=(1,),
            in_specs=[narrow(0), wide(1), wide(2), narrow(3), part, part],
            out_specs=(part, part, sums, sums, whole(rows, depth, width)),
            scratch_shapes=[
                pltpu.VMEM((groups, 2, 8, length), F32),
                pltpu.VMEM((groups, 2, 8, length), F32),
                pltpu.VMEM((2, width, length), F32),
                pltpu.VMEM((2, width, length), F32),
                pltpu.VMEM((2, width, length), BF),
                pltpu.VMEM((2, width, length), BF),
            ],
        ),
        out_shape=(
            jax.ShapeDtypeStruct((groups, 8, length), F32),
            jax.ShapeDtypeStruct((groups, 8, length), BF),
            jax.ShapeDtypeStruct((rows, depth, length), F32),
            jax.ShapeDtypeStruct((rows, depth, length), F32),
            jax.ShapeDtypeStruct((rows, depth, width), BF),
        ),
        compiler_params=pltpu.CompilerParams(vmem_limit_bytes=24 * 1024 * 1024),
        cost_estimate=pl.CostEstimate(flops=COST, bytes_accessed=4_000_000, transcendentals=0),
        name="attention_chunk",
    )(place, qkvg, qkvg, qkvg, qkvg, mine, sibling)


def gather_kernel(scale, starts, *refs):
    out = refs[-1]
    chunks = (len(refs) - 1) // 3
    gk, gv, gq = refs[:chunks], refs[chunks : 2 * chunks], refs[2 * chunks : 3 * chunks]
    width = gq[0].shape[-1]
    for r in range(out.shape[1]):
        for i in range(chunks):
            out[0, r, :, pl.ds(pl.multiple_of(starts[i] * width, width), width)] = gq[i][r]
        sum_k, sum_v = gk[0][r], gv[0][r]
        for i in range(1, chunks):
            sum_k, sum_v = sum_k + gk[i][r], sum_v + gv[i][r]
        out[1, r] = (sum_k * scale).astype(BF)
        out[2, r] = sum_v.astype(BF)


def gather_gradients(starts, gk, gv, gq, scale):
    rows, depth, length = gk[0].shape
    return pl.pallas_call(
        functools.partial(gather_kernel, scale),
        in_specs=[pl.BlockSpec(memory_space=pltpu.SMEM)]
        + [pl.BlockSpec(memory_space=pltpu.VMEM)] * (3 * len(gk)),
        out_specs=pl.BlockSpec(memory_space=pltpu.VMEM),
        out_shape=jax.ShapeDtypeStruct((3, rows, depth, length), BF),
        compiler_params=pltpu.CompilerParams(vmem_limit_bytes=16 * 1024 * 1024),
        name="gather_gradients",
    )(starts, *gk, *gv, *gq)


def plane_kernel(own, got, one, two, three, out):
    half = out.shape[-1]
    for n in range(out.shape[0]):
        s = own[n] + got[n].astype(F32)
        s = s + one[n].astype(F32) + two[n].astype(F32) + three[n].astype(F32)
        low = s.astype(BF)
        for h in range(NH):
            out[n, h] = low[:, h * half : (h + 1) * half]


def plane_sum(own, got, arrived):
    groups, eight, length = own.shape
    return pl.pallas_call(
        plane_kernel,
        out_shape=jax.ShapeDtypeStruct((groups, NH, eight, length // NH), BF),
        compiler_params=pltpu.CompilerParams(vmem_limit_bytes=8 * 1024 * 1024),
        name="plane_sum",
    )(own, got, *arrived)


def pair_kernel(terms, weight, out):
    width = terms.shape[-1]
    heads = []
    for y in range(NY):
        for h in range(NH):
            s = terms[0, y, h].astype(F32)
            for z in range(1, NZ):
                s = s + terms[z, y, h].astype(F32)
            heads.append(split3(s))
    pad = jnp.zeros((4, width), F32)
    for j in range(out.shape[0]):
        lhs = [heads[i][p][j : j + 1, :].astype(F32) for p in range(3) for i in range(4)]
        lhs = jnp.concatenate(lhs + [pad], axis=0).astype(BF)
        out[j] = lax.dot_general(lhs, weight[...], OVER_ROWS, preferred_element_type=F32).astype(BF)


def pair_gradient(terms, weight):
    return pl.pallas_call(
        pair_kernel,
        out_shape=jax.ShapeDtypeStruct((terms.shape[3], terms.shape[4], weight.shape[1]), BF),
        compiler_params=pltpu.CompilerParams(vmem_limit_bytes=8 * 1024 * 1024),
        name="pair_gradient",
    )(terms, weight)


def shards(queries, keys, values, d_out, bias, w_bias):
    _, _, depth, length = queries.shape
    scale = depth ** (-0.5)
    x, y, c = lax.axis_index("x"), lax.axis_index("yh"), lax.axis_index("core")

    all_in = (queries, keys, values, d_out)
    pick = lambda at: jnp.stack([lax.dynamic_index_in_dim(t, at, 1, keepdims=False) for t in all_in])
    got_in = shift(pick(1 - y), "yh", NY, 1)

    spread = jnp.broadcast_to(bias[None], (NZ,) + bias.shape).reshape(NZ * NY, 8, length)
    own_bias = lax.all_to_all(spread, ("z", "yh"), 0, 0, tiled=True)
    own_bias, got_in = lax.optimization_barrier((own_bias, got_in))
    qkvg = jnp.concatenate([pick(y), got_in], axis=1)
    order = (0, 1, 3, 2)
    halves = [shift(own_bias, "x", NX, dx) if dx else own_bias for dx in order]

    parts = []
    arrived = []
    for at, dx in enumerate(order):
        mine = halves[at]
        if at == 1:
            mine = lax.optimization_barrier((mine, plane_own))[0]
        sibling = shift(mine, "core", NC, 1)
        place = jnp.stack([(x + NX - dx) % NX, c]).astype(jnp.int32)
        own, other, *grads = chunk(place, qkvg, mine, sibling, scale)
        parts.append(grads)
        got = shift(other, "core", NC, 1)
        if dx:
            arrived.append(shift((own + got.astype(F32)).astype(BF), "x", NX, -dx))
        else:
            plane_own, plane_got = own, got
    starts = jnp.stack([(x + NX - dx) % NX for dx in order]).astype(jnp.int32)
    grads = gather_gradients(starts, *zip(*parts), scale)

    plane = plane_sum(plane_own, plane_got, arrived)
    plane = plane.reshape(NZ * NY * NH, 8, length // NH)
    terms = lax.all_to_all(plane, ("z", "yh", "heads"), 0, 0, tiled=True)
    terms = terms.reshape(NZ, NY, NH, 8, length // NH)
    weight = jnp.stack([w_bias[:, 2 * h + y] for y in range(NY) for h in range(NH)])
    weight = jnp.concatenate([weight, weight, weight, jnp.zeros_like(weight)], axis=0)
    d_pair = pair_gradient(terms, weight)

    back = shift(grads[:, 2:], "yh", NY, 1)
    mine = grads[:, :2]
    first = jnp.where(y == 0, mine, back)
    second = jnp.where(y == 0, back, mine)
    outs = jnp.stack([first, second], axis=2)
    return outs[0], outs[1], outs[2], d_pair


def solution(mesh):
    fine = Mesh(mesh.devices.reshape(NX, NZ, NY, NC, NH), GRID)
    block = P(ROWS, "heads", None, None)
    return jax.shard_map(
        shards,
        mesh=fine,
        in_specs=(block, block, block, block, P("heads", ROWS, None), P()),
        out_specs=(block, block, block, P(ROWS, "heads", None)),
        check_vma=False,
    )
```

```python
import functools

import jax
import jax.numpy as jnp
from jax import lax
from jax.experimental import pallas as pl
from jax.experimental.pallas import tpu as pltpu
from jax.sharding import Mesh, PartitionSpec as P

NX, NZ, NY, NC, NH = 4, 8, 2, 2, 2
GRID = ("x", "z", "yh", "core", "heads")
ROWS = ("x", "z", "yh", "core")
COST = 500_000_000
LOG2E = 1.4426950408889634
BF = jnp.bfloat16
F32 = jnp.float32
OVER_ROWS = (((0,), (0,)), ((), ()))
OVER_COLS = (((1,), (1,)), ((), ()))


def shift(value, axis, size, by):
    return lax.ppermute(value, axis, [(i, (i + by) % size) for i in range(size)])


def split3(value):
    hi = value.astype(BF)
    rest = value - hi.astype(F32)
    mid = rest.astype(BF)
    low = (rest - mid.astype(F32)).astype(BF)
    return hi, mid, low


def chunk_kernel(scale, place, q_ref, k_ref, v_ref, g_ref, q2_ref, k2_ref, v2_ref, g2_ref, bias,
                 out, gk_ref, gv_ref, gq_ref, bias_f, total, s_buf, p_buf, pl_buf, dl_buf, qs, gs):
    near, depth, width = q_ref.shape[1:]
    rows = 2 * near
    length = k_ref.shape[-1]
    tiles = length // 256
    half = width // 2
    strips = half // 16
    groups = half // 8

    position = lax.broadcasted_iota(jnp.int32, (width, half), 0)
    column = lax.broadcasted_iota(jnp.int32, (width, half), 1)
    wanted = 16 * lax.shift_right_logical(column, 3) + (column & 7) + 8 * place[1]
    pick = jnp.where(position == wanted, 1.0, 0.0).astype(BF)
    for at, (q, g) in enumerate(((q_ref, g_ref), (q2_ref, g2_ref))):
        for src, dst in ((q, qs), (g, gs)):
            low = jnp.dot(src[0].reshape(near * depth, width), pick, preferred_element_type=F32).astype(BF)
            dst[at * near : (at + 1) * near] = low.reshape(near, depth, half)
    k_at = lambda r, cols=slice(None): (k_ref if r < near else k2_ref)[0, r % near, :, cols]
    v_at = lambda r, cols=slice(None): (v_ref if r < near else v2_ref)[0, r % near, :, cols]

    for n in range(groups):
        bias_f[8 * n : 8 * n + 8, :] = bias[n].astype(F32) * LOG2E

    held = {}

    def scores(r, t):
        if t == 0:
            q3 = jnp.concatenate(split3(qs[r].astype(F32) * (scale * LOG2E)), axis=0)
            k = k_at(r)
            held[r] = (q3, jnp.concatenate([k, k, k], axis=0))
        cols = slice(256 * (t % tiles), 256 * (t % tiles) + 256)
        if t < tiles:
            s_buf[r % 2, :, cols] = lax.dot_general(
                held[r][0], held[r][1][:, cols], OVER_ROWS, preferred_element_type=F32
            )
        else:
            p_buf[r % 2, :, cols] = lax.dot_general(
                gs[r], v_at(r, cols), OVER_ROWS, preferred_element_type=F32
            )

    sums = {}

    def gradients(r, t):
        cols = slice(256 * (t % tiles), 256 * (t % tiles) + 256)
        if t < tiles:
            gk_ref[r, :, cols] = jnp.dot(qs[r], dl_buf[r % 2, :, cols], preferred_element_type=F32)
        elif t < 2 * tiles:
            gv_ref[r, :, cols] = jnp.dot(gs[r], pl_buf[r % 2, :, cols], preferred_element_type=F32)
        else:
            new = lax.dot_general(
                k_at(r, cols), dl_buf[r % 2, :, cols], OVER_COLS, preferred_element_type=F32
            )
            sums[r] = sums[r] + new if r in sums else new
            if t == 3 * tiles - 1:
                low = (sums[r] * scale).astype(BF)
                gq_ref[r] = lax.dot_general(low, pick, OVER_COLS, preferred_element_type=F32).astype(BF)

    def softmax(r, n):
        here = slice(16 * n, 16 * n + 16)
        s = s_buf[r % 2, here, :] + bias_f[here, :]
        top = jnp.max(s, axis=1, keepdims=True)
        expo = jnp.exp2(s - top)
        inv = 1.0 / jnp.sum(expo, axis=1, keepdims=True)
        dp = p_buf[r % 2, here, :]
        mean = jnp.sum(expo * dp, axis=1, keepdims=True) * inv
        probs = expo * inv
        ds = probs * (dp - mean)
        pl_buf[r % 2, here, :] = probs.astype(BF)
        dl_buf[r % 2, here, :] = ds.astype(BF)
        if r == 0:
            total[here, :] = ds
        else:
            total[here, :] += ds

    for step in range(rows + 2):
        matmuls = []
        if step < rows:
            matmuls += [(scores, step, t) for t in range(2 * tiles)]
        if step >= 2:
            matmuls += [(gradients, step - 2, t) for t in range(3 * tiles)]
        if 0 <= step - 1 < rows:
            for n in range(strips):
                for f, r, t in matmuls[len(matmuls) * n // strips : len(matmuls) * (n + 1) // strips]:
                    f(r, t)
                softmax(step - 1, n)
        else:
            for f, r, t in matmuls:
                f(r, t)

    for n in range(groups):
        out[n] = total[8 * n : 8 * n + 8, :].astype(out.dtype)


def chunk(place, mine, sibling, bias, out_type, scale):
    _, near, depth, length = mine.shape
    groups = bias.shape[0]
    half = 8 * groups
    width = 2 * half
    rows = 2 * near
    narrow = lambda i: pl.BlockSpec((1, near, depth, width), lambda g, p: (i, 0, 0, p[0]))
    wide = lambda i: pl.BlockSpec((1, near, depth, length), lambda g, p: (i, 0, 0, 0))
    whole = lambda *shape: pl.BlockSpec(shape, lambda g, p: (0,) * len(shape))
    part = whole(groups, 8, length)
    sums = whole(rows, depth, length)
    return pl.pallas_call(
        functools.partial(chunk_kernel, scale),
        grid_spec=pltpu.PrefetchScalarGridSpec(
            num_scalar_prefetch=1,
            grid=(1,),
            in_specs=[narrow(0), wide(1), wide(2), narrow(3)] * 2 + [part],
            out_specs=(part, sums, sums, whole(rows, depth, width)),
            scratch_shapes=[
                pltpu.VMEM((half, length), F32),
                pltpu.VMEM((half, length), F32),
                pltpu.VMEM((2, half, length), F32),
                pltpu.VMEM((2, half, length), F32),
                pltpu.VMEM((2, half, length), BF),
                pltpu.VMEM((2, half, length), BF),
                pltpu.VMEM((rows, depth, half), BF),
                pltpu.VMEM((rows, depth, half), BF),
            ],
        ),
        out_shape=(
            jax.ShapeDtypeStruct((groups, 8, length), out_type),
            jax.ShapeDtypeStruct((rows, depth, length), F32),
            jax.ShapeDtypeStruct((rows, depth, length), F32),
            jax.ShapeDtypeStruct((rows, depth, width), BF),
        ),
        compiler_params=pltpu.CompilerParams(vmem_limit_bytes=24 * 1024 * 1024),
        cost_estimate=pl.CostEstimate(flops=COST, bytes_accessed=500_000, transcendentals=0),
        name="attention_chunk",
    )(place, *[mine] * 4, *[sibling] * 4, bias)


def gather_kernel(starts, *refs):
    own, other, own_q, other_q = refs[-4:]
    chunks = (len(refs) - 4) // 3
    gk, gv, gq = refs[:chunks], refs[chunks : 2 * chunks], refs[2 * chunks : 3 * chunks]
    width = gq[0].shape[-1]
    near = own.shape[1]
    for r in range(2 * near):
        out, out_q = (own, own_q) if r < near else (other, other_q)
        for i in range(chunks):
            out_q[r % near, :, pl.ds(pl.multiple_of(starts[i] * width, width), width)] = gq[i][r]
        for at, terms in enumerate((gk, gv)):
            s = terms[0][r]
            for i in range(1, chunks):
                s = s + terms[i][r]
            out[at, r % near] = s


def gather_gradients(starts, gk, gv, gq):
    rows, depth, length = gk[0].shape
    sums = jax.ShapeDtypeStruct((2, rows // 2, depth, length), F32)
    queries = jax.ShapeDtypeStruct((rows // 2, depth, length), BF)
    return pl.pallas_call(
        gather_kernel,
        in_specs=[pl.BlockSpec(memory_space=pltpu.SMEM)]
        + [pl.BlockSpec(memory_space=pltpu.VMEM)] * (3 * len(gk)),
        out_specs=[pl.BlockSpec(memory_space=pltpu.VMEM)] * 4,
        out_shape=(sums, sums, queries, queries),
        compiler_params=pltpu.CompilerParams(vmem_limit_bytes=20 * 1024 * 1024),
        name="gather_gradients",
    )(starts, *gk, *gv, *gq)


def join_kernel(scale, own, got, own_q, got_q, out):
    for r in range(out.shape[1]):
        out[0, r] = (own_q[r].astype(F32) + got_q[r].astype(F32)).astype(BF)
        out[1, r] = ((own[0, r] + got[0, r]) * scale).astype(BF)
        out[2, r] = (own[1, r] + got[1, r]).astype(BF)


def join_gradients(own, got, own_q, got_q, scale):
    return pl.pallas_call(
        functools.partial(join_kernel, scale),
        out_shape=jax.ShapeDtypeStruct((3,) + own_q.shape, BF),
        compiler_params=pltpu.CompilerParams(vmem_limit_bytes=8 * 1024 * 1024),
        name="join_gradients",
    )(own, got, own_q, got_q)


def place_kernel(place, grads, back, *outs):
    y = place[0]
    for at, out in enumerate(outs):
        for r in range(out.shape[0]):
            out[r, y] = grads[at, r]
            out[r, 1 - y] = back[at, r]


def place_gradients(place, grads, back):
    _, rows, depth, length = back.shape
    block = pl.BlockSpec((3, rows, depth, length), lambda g, p: (0, 0, 0, 0))
    return pl.pallas_call(
        place_kernel,
        grid_spec=pltpu.PrefetchScalarGridSpec(
            num_scalar_prefetch=1,
            grid=(1,),
            in_specs=[block, block],
            out_specs=[pl.BlockSpec((rows, NH, depth, length), lambda g, p: (0, 0, 0, 0))] * 3,
        ),
        out_shape=[jax.ShapeDtypeStruct((rows, NH, depth, length), BF)] * 3,
        compiler_params=pltpu.CompilerParams(vmem_limit_bytes=8 * 1024 * 1024),
        name="place_gradients",
    )(place, grads, back)


def plane_kernel(own, one, two, three, out):
    half = out.shape[-1]
    for n in range(out.shape[0]):
        s = own[n] + one[n].astype(F32) + two[n].astype(F32) + three[n].astype(F32)
        low = s.astype(BF)
        for h in range(NH):
            out[n, h] = low[:, h * half : (h + 1) * half]


def plane_sum(own, arrived):
    groups, eight, length = own.shape
    return pl.pallas_call(
        plane_kernel,
        out_shape=jax.ShapeDtypeStruct((groups, NH, eight, length // NH), BF),
        compiler_params=pltpu.CompilerParams(vmem_limit_bytes=8 * 1024 * 1024),
        name="plane_sum",
    )(own, *arrived)


def pair_kernel(terms, weight, out):
    width = terms.shape[-1]
    heads = []
    for y in range(NY):
        for h in range(NH):
            s = terms[0, y, h].astype(F32)
            for z in range(1, NZ):
                s = s + terms[z, y, h].astype(F32)
            heads.append(split3(s))
    pad = jnp.zeros((4, width), F32)
    for j in range(out.shape[0]):
        lhs = [heads[i][p][j : j + 1, :].astype(F32) for p in range(3) for i in range(4)]
        lhs = jnp.concatenate(lhs + [pad], axis=0).astype(BF)
        out[j] = lax.dot_general(lhs, weight[...], OVER_ROWS, preferred_element_type=F32).astype(BF)


def pair_gradient(terms, weight):
    return pl.pallas_call(
        pair_kernel,
        out_shape=jax.ShapeDtypeStruct((terms.shape[3], terms.shape[4], weight.shape[1]), BF),
        compiler_params=pltpu.CompilerParams(vmem_limit_bytes=8 * 1024 * 1024),
        name="pair_gradient",
    )(terms, weight)


def shards(queries, keys, values, d_out, bias, w_bias):
    _, _, depth, length = queries.shape
    scale = depth ** (-0.5)
    x, y, c = lax.axis_index("x"), lax.axis_index("yh"), lax.axis_index("core")

    all_in = (queries, keys, values, d_out)
    pick = lambda at: jnp.stack([lax.dynamic_index_in_dim(t, at, 1, keepdims=False) for t in all_in])
    got_in = shift(pick(1 - y), "yh", NY, 1)

    spread = jnp.broadcast_to(bias[None], (NZ,) + bias.shape).reshape(NZ * NY, 8, length)
    own_bias = lax.all_to_all(spread, ("z", "yh"), 0, 0, tiled=True)
    own_bias, got_in = lax.optimization_barrier((own_bias, got_in))
    qkvg = jnp.concatenate([pick(y), got_in], axis=1)
    sibling = shift(qkvg, "core", NC, 1)
    order = (0, 1, 3, 2)
    biases = [shift(own_bias, "x", NX, dx) if dx else own_bias for dx in order]

    parts = []
    arrived = []
    for at, dx in enumerate(order):
        place = jnp.stack([(x + NX - dx) % NX, c]).astype(jnp.int32)
        if at:
            place = lax.optimization_barrier((place, out))[0]
        out, *grads = chunk(place, qkvg, sibling, biases[at], BF if dx else F32, scale)
        parts.append(grads)
        if dx:
            arrived.append(shift(out, "x", NX, -dx))
        else:
            own = out
    starts = jnp.stack([(x + NX - dx) % NX for dx in order]).astype(jnp.int32)
    starts = lax.optimization_barrier((starts, *arrived[:2]))[0]
    ours, theirs, ours_q, theirs_q = gather_gradients(starts, *zip(*parts))
    got, got_q = shift(theirs, "core", NC, 1), shift(theirs_q, "core", NC, 1)
    grads = join_gradients(ours, got, ours_q, got_q, scale)

    back = shift(grads[:, 2:], "yh", NY, 1)

    plane, back = lax.optimization_barrier((plane_sum(own, arrived), back))
    plane = plane.reshape(NZ * NY * NH, 8, length // NH)
    terms = lax.all_to_all(plane, ("z", "yh", "heads"), 0, 0, tiled=True)
    terms = terms.reshape(NZ, NY, NH, 8, length // NH)
    outs = place_gradients(jnp.stack([y]).astype(jnp.int32), grads, back)
    terms, *outs = lax.optimization_barrier((terms, *outs))
    weight = jnp.stack([w_bias[:, 2 * h + y] for y in range(NY) for h in range(NH)])
    weight = jnp.concatenate([weight, weight, weight, jnp.zeros_like(weight)], axis=0)
    d_pair = pair_gradient(terms, weight)
    return (*outs, d_pair)


def solution(mesh):
    fine = Mesh(mesh.devices.reshape(NX, NZ, NY, NC, NH), GRID)
    block = P(ROWS, "heads", None, None)
    return jax.shard_map(
        shards,
        mesh=fine,
        in_specs=(block, block, block, block, P("heads", ROWS, None), P()),
        out_specs=(block, block, block, P(ROWS, "heads", None)),
        check_vma=False,
    )
```
